32 devices in a mesh: blk: 32 (over z, y, x, core).
Axes of the slice: x: 2, y: 2, z: 4, core: 2. Of those that a mesh axis runs over, the one named last changes fastest.
Arguments:
- features: float32 [8192, 128], P('blk'), may hold values from -6 to 6
- weight_one: float32 [128, 128], replicated, may hold values from -0.5 to 0.5
- weight_two: float32 [128, 128], replicated, may hold values from -0.5 to 0.5
- dense_tiles: bfloat16 [1024, 128, 128], P('blk'), may hold values from -0.078125 to 0.078125
- dense_row: int32 [1024], P('blk'), may hold values from 0 to 1
- hub_block: int32 [32], replicated, may hold values from 0 to 1
- sparse_tiles: bfloat16 [3584, 128, 128], P('blk'), may hold values from -0.078125 to 0.078125
- sparse_row: int32 [3584], P('blk'), may hold values from 0 to 1
- sparse_src: int32 [3584], P('blk'), may hold values from 0 to 5
- sparse_count: int32 [32], P('blk'), may hold values from 1 to 112, as said below
- fetch_list: int32 [32, 4], P('blk'), may hold values from 0 to 1
Outputs:
- embedded: float32 [8192, 128], P('blk')
The draws below stay inside these ranges and needn't reach their ends.
Inputs may be any that keep to these rules, and one draw needn't show every extreme that they name: `sparse_count`: one device has exactly 112 live slots.
All inputs are finite; a program needn't handle non-finite values.
Results may differ from the reference program's by a relative error of at most 0.0041.
Values may be sent and summed in bfloat16 or wider, within the bound.
A program may use at most 128 MiB of HBM per device.

```python
import jax
import jax.numpy as jnp
from jax import lax

F = 128
TILE = 128
NB = 2
KS = 112
HOPS = 2
FETCH = 1
NODES = 8192
N_BLK = 32


def draw_sparse_count(key, part):
    first_key, second_key = jax.random.split(jax.random.fold_in(key, 7))
    levels = jax.random.randint(first_key, (N_BLK,), 0, 16)
    counts = jnp.maximum(KS * levels * levels // 225, KS // 16 + 1)
    busiest = jax.random.randint(second_key, (), 0, N_BLK)
    counts = jnp.where(jnp.arange(N_BLK) == busiest, KS, counts)
    return counts.astype(jnp.int32)


def set_ends(values, rng, low, top_value):
    dims = values.shape
    index_at = [jax.random.randint(jax.random.fold_in(rng, axis), (), 0, dims[axis]) for axis in range(len(dims))]
    values = values.at[tuple(index_at)].set(low)
    longest = dims.index(max(dims))
    index_at[longest] = (index_at[longest] + 1) % dims[longest]
    return values.at[tuple(index_at)].set(top_value)


def shard_levels(own_key, shape, cuts, smallest, high):
    def one(position, shards_of):
        draws = jax.random.uniform(jax.random.fold_in(jax.random.fold_in(own_key, 6), position), (shards_of,), jnp.float32, smallest / len(cuts), high / len(cuts))
        return jnp.repeat(jnp.exp(draws), shape[position] // shards_of).reshape((-1,) + (1,) * (len(shape) - position - 1))

    level = one(*cuts[0])
    for cut in cuts[1:]:
        level = level * one(*cut)
    return level


def centred(key, shape, width, limit, cuts=(), kind=jnp.bfloat16):
    entries = width * jax.random.normal(key, shape, jnp.float32)
    if cuts:
        entries = entries * shard_levels(key, shape, cuts, -0.22, 0.18)
    return jnp.clip(entries, -limit, limit).astype(kind)


def setup_inputs(seed: int = 0) -> dict:
    arg_keys = jax.random.split(jax.random.key(seed), 12)
    features = centred(arg_keys[0], (NODES, F), 1.0, 6.0, ((0, 32),), jnp.float32)
    weight_one = centred(arg_keys[1], (F, F), F ** -0.5, 0.5, (), jnp.float32)
    weight_two = centred(arg_keys[2], (F, F), F ** -0.5, 0.5, (), jnp.float32)
    dense_tiles = centred(arg_keys[3], (N_BLK * N_BLK, TILE, TILE), (TILE * (N_BLK // NB + KS // (2 * NB))) ** -0.5, 0.078125, ((0, 32),))
    dense_row = set_ends(jax.random.randint(arg_keys[4], (N_BLK * N_BLK,), 0, NB), jax.random.fold_in(arg_keys[4], 1), 0, NB - 1).astype(jnp.int32)
    hub_block = set_ends(jax.random.randint(arg_keys[5], (N_BLK,), 0, NB), jax.random.fold_in(arg_keys[5], 1), 0, NB - 1).astype(jnp.int32)
    sparse_tiles = centred(arg_keys[6], (N_BLK * KS, TILE, TILE), (TILE * (N_BLK // NB + KS // (2 * NB))) ** -0.5, 0.078125, ((0, 32),))
    sparse_row = set_ends(jax.random.randint(arg_keys[7], (N_BLK * KS,), 0, NB), jax.random.fold_in(arg_keys[7], 1), 0, NB - 1).astype(jnp.int32)
    sparse_src = set_ends(jax.random.randint(arg_keys[8], (N_BLK * KS,), 0, NB + 2 * HOPS * FETCH), jax.random.fold_in(arg_keys[8], 1), 0, (NB + 2 * HOPS * FETCH) - 1).astype(jnp.int32)
    sparse_count = draw_sparse_count(jax.random.fold_in(arg_keys[11], 71), 0)
    fetch_list = set_ends(jax.random.randint(arg_keys[10], (N_BLK, 2 * HOPS * FETCH), 0, NB), jax.random.fold_in(arg_keys[10], 1), 0, NB - 1).astype(jnp.int32)
    return {"features": features, "weight_one": weight_one, "weight_two": weight_two, "dense_tiles": dense_tiles, "dense_row": dense_row, "hub_block": hub_block, "sparse_tiles": sparse_tiles, "sparse_row": sparse_row, "sparse_src": sparse_src, "sparse_count": sparse_count, "fetch_list": fetch_list}


def neighbour_offsets():
    return list(range(-HOPS, 0)) + list(range(1, HOPS + 1))


def reference(features, weight_one, weight_two, dense_tiles, dense_row, hub_block, sparse_tiles, sparse_row, sparse_src, sparse_count, fetch_list):
    offsets = neighbour_offsets()
    owner_shift = jnp.array([offsets[entry // FETCH] for entry in range(2 * HOPS * FETCH)], dtype=jnp.int32)
    block_ids = jnp.arange(NB, dtype=jnp.int32)
    slot_ids = jnp.arange(KS, dtype=jnp.int32)
    device_ids = jnp.arange(N_BLK, dtype=jnp.int32)

    def propagate(hidden_rows, weight):
        blocks = hidden_rows.reshape(N_BLK, NB, TILE, F)
        hub_rows = blocks[device_ids, hub_block].astype(jnp.float32)

        def one_device(device):
            dense_start = (device * N_BLK).astype(jnp.int32)
            tile_set = lax.dynamic_slice_in_dim(dense_tiles, dense_start, N_BLK, 0).astype(jnp.float32)
            row_ids = lax.dynamic_slice_in_dim(dense_row, dense_start, N_BLK, 0)
            products = jnp.einsum("sij,sjf->sif", tile_set, hub_rows)
            onehot = (row_ids[:, None] == block_ids[None, :]).astype(jnp.float32)
            summed = jnp.einsum("sn,sif->nif", onehot, products, precision=lax.Precision.HIGHEST)
            owners = ((device + owner_shift) % N_BLK).astype(jnp.int32)
            wanted = lax.dynamic_index_in_dim(fetch_list, device, 0, keepdims=False)
            fetched = blocks[owners, wanted]
            own_blocks = lax.dynamic_index_in_dim(blocks, device, 0, keepdims=False)
            gathered_blocks = jnp.concatenate([own_blocks, fetched], axis=0)
            sparse_start = (device * KS).astype(jnp.int32)
            sparse_set = lax.dynamic_slice_in_dim(sparse_tiles, sparse_start, KS, 0).astype(jnp.float32)
            sparse_rows = lax.dynamic_slice_in_dim(sparse_row, sparse_start, KS, 0)
            sources = lax.dynamic_slice_in_dim(sparse_src, sparse_start, KS, 0)
            inputs = gathered_blocks[sources].astype(jnp.float32)
            sparse_products = jnp.einsum("kij,kjf->kif", sparse_set, inputs)
            live_total = lax.dynamic_index_in_dim(sparse_count, device, 0, keepdims=False)
            live_mask = (slot_ids < live_total).astype(jnp.float32)
            sparse_onehot = (sparse_rows[:, None] == block_ids[None, :]).astype(jnp.float32) * live_mask[:, None]
            summed = summed + jnp.einsum("kn,kif->nif", sparse_onehot, sparse_products, precision=lax.Precision.HIGHEST)
            return summed.reshape(NB * TILE, F)

        summed_all = lax.map(one_device, device_ids)
        projected = jnp.dot(summed_all.reshape(N_BLK * NB * TILE, F), weight, precision=lax.Precision.HIGHEST, preferred_element_type=jnp.float32)
        return jax.nn.relu(projected)

    inputs_first = features.astype(jnp.bfloat16)
    hidden = propagate(inputs_first, weight_one).astype(jnp.bfloat16)
    return propagate(hidden, weight_two)
```

```python
import functools
import math

import jax
import jax.numpy as jnp
from jax import lax
from jax.experimental import pallas as pl
from jax.experimental.pallas import tpu as pltpu
from jax.sharding import PartitionSpec as P

F = 128
TILE = 128
HOPS = 2
OFFSETS = list(range(-HOPS, 0)) + list(range(1, HOPS + 1))
MESH = pl.DeviceIdType.MESH
BF16 = jnp.bfloat16
F32 = jnp.float32


def plane_side(chips):
    side = 1
    while chips % ((2 * side) ** 2) == 0 and 2 * (2 * side) ** 3 <= chips:
        side *= 2
    return side


def kernel(
    size, slots,
    dense_row, hub_block, sparse_row, sparse_src, sparse_count, fetch_list,
    features, weight_one, weight_two, dense_hbm, sparse_hbm,
    out,
    feat, weights, dense, sparse, own, spare, stripe, fetched, table, acc,
    load_sem, send_sem, recv_sem, near_send, near_recv,
):
    side = plane_side(size // 2)
    long = size // (2 * side * side)
    me = lax.axis_index("blk")
    core = me % 2
    x = (me // 2) % side
    y = (me // (2 * side)) % side
    z = me // (2 * side * side)
    z_stride = 2 * side * side
    a = x + core * (y - x)
    b = y + core * (x - y)
    a_stride = 2 + core * (2 * side - 2)
    b_stride = 2 * side + core * (2 - 2 * side)

    def at(da, db, dz, other=0):
        return (
            me
            + ((a + da) % side - a) * a_stride
            + ((b + db) % side - b) * b_stride
            + ((z + dz) % long - z) * z_stride
            + other * (1 - 2 * core)
        )

    z_peers = [at(0, 0, k) for k in range(1, long)]
    a_peers = [at(k, 0, 0) for k in range(1, side)]
    b_peers = [at(0, k, 0) for k in range(1, side)]
    twin = at(0, 0, 0, 1)
    owners = [(me + offset + size) % size for offset in OFFSETS]
    readers = [(me - offset + size) % size for offset in OFFSETS]

    barrier = pltpu.get_barrier_semaphore()
    partners = z_peers + a_peers + b_peers + [twin] + owners
    for peer in partners:
        pl.semaphore_signal(barrier, inc=1, device_id=(peer,), device_id_type=MESH)

    loads = [
        pltpu.make_async_copy(features, feat, load_sem.at[0]),
        pltpu.make_async_copy(dense_hbm, dense, load_sem.at[1]),
        pltpu.make_async_copy(sparse_hbm, sparse, load_sem.at[2]),
        pltpu.make_async_copy(weight_one, weights.at[0], load_sem.at[3]),
        pltpu.make_async_copy(weight_two, weights.at[1], load_sem.at[4]),
    ]
    for load in loads:
        load.start()

    table[...] = jnp.zeros_like(table)
    hub_here = hub_block[me]
    live = sparse_count[0]
    dead_key = table.shape[0] - 1
    group = math.gcd(slots, 8)

    loads[0].wait()
    for layer in range(2):
        if layer == 0:
            rows = feat[...].astype(BF16)
        first, second = rows[:TILE], rows[TILE:]
        stripe[layer, me] = jnp.where(hub_here == 0, first, second)
        spare[layer] = jnp.where(hub_here == 0, second, first)
        own[0] = first
        own[1] = second
        if layer == 0:
            pl.semaphore_wait(barrier, len(partners))

        def copy(block, peer):
            return pltpu.make_async_remote_copy(
                src_ref=stripe.at[layer, block],
                dst_ref=stripe.at[layer, block],
                send_sem=send_sem.at[layer],
                recv_sem=recv_sem.at[layer, block],
                device_id=(peer,),
                device_id_type=MESH,
            )

        def near(entry):
            return pltpu.make_async_remote_copy(
                src_ref=spare.at[layer],
                dst_ref=fetched.at[layer, entry],
                send_sem=near_send.at[layer, entry],
                recv_sem=near_recv.at[layer, entry],
                device_id=(readers[entry],),
                device_id_type=MESH,
            )

        def arrive(block):
            copy(block, twin).wait_recv()

        def dense_group(da, db, other):
            blocks = [at(da, db, dz, other) for dz in range(long)]
            left = jnp.concatenate([dense[block] for block in blocks], axis=1)
            right = []
            for block in blocks:
                held = stripe[layer, block]
                row = dense_row[block]
                blank = jnp.zeros_like(held)
                right.append(
                    jnp.concatenate(
                        [jnp.where(row == 0, held, blank), jnp.where(row == 1, held, blank)], axis=1
                    )
                )
            acc[...] += jnp.dot(left, jnp.concatenate(right, axis=0), preferred_element_type=F32)

        for peer in a_peers + b_peers + z_peers + [twin]:
            copy(me, peer).start()
        for entry in range(len(OFFSETS)):
            near(entry).start()
        for source in (0, 1):
            for row in (0, 1):
                table[2 * source + row, :, row * F : (row + 1) * F] = own[source]
        acc[...] = jnp.zeros_like(acc)

        def from_a(da, dz):
            block = at(da, 0, dz)
            arrive(block)
            for peer in b_peers + [twin]:
                copy(block, peer).start()

        for da in range(1, side):
            from_a(da, 0)

        @pl.loop(1, long)
        def _(dz):
            block = at(0, 0, dz)
            arrive(block)
            for peer in a_peers + b_peers + [twin]:
                copy(block, peer).start()

        for da in range(1, side):

            @pl.loop(1, long)
            def _(dz):
                from_a(da, dz)

        if layer == 0:
            loads[1].wait()
        dense_group(0, 0, 0)
        for db in range(1, side):
            for da in range(side):

                @pl.loop(0, long)
                def _(dz):
                    block = at(da, db, dz)
                    arrive(block)
                    copy(block, twin).start()

        for da in range(1, side):
            dense_group(da, 0, 0)
        for db in range(1, side):
            for da in range(side):
                dense_group(da, db, 0)

        for db in range(side):
            for da in range(side):

                @pl.loop(0, long)
                def _(dz):
                    arrive(at(da, db, dz, 1))

                dense_group(da, db, 1)

        for entry in range(len(OFFSETS)):
            near(entry).wait_recv()
            owner = owners[entry]
            block = jnp.where(
                fetch_list[0, entry] == hub_block[owner], stripe[layer, owner], fetched[layer, entry]
            )
            for row in (0, 1):
                table[2 * (entry + 2) + row, :, row * F : (row + 1) * F] = block
        if layer == 0:
            loads[2].wait()

        @pl.loop(0, slots // group)
        def _(step):
            left, right = [], []
            for inner in range(group):
                slot = step * group + inner
                key = jnp.where(slot < live, 2 * sparse_src[slot] + sparse_row[slot], dead_key)
                left.append(sparse[slot])
                right.append(table[key])
            acc[...] += jnp.dot(
                jnp.concatenate(left, axis=1),
                jnp.concatenate(right, axis=0),
                preferred_element_type=F32,
            )

        if layer == 0:
            loads[3].wait()
            loads[4].wait()
        summed = jnp.concatenate([acc[:, :F], acc[:, F:]], axis=0)
        weight = weights[layer]
        high = summed.astype(BF16)
        low = (summed - high.astype(F32)).astype(BF16)
        weight_high = weight.astype(BF16)
        weight_low = (weight - weight_high.astype(F32)).astype(BF16)
        projected = jnp.dot(
            jnp.concatenate([high, low, high], axis=1),
            jnp.concatenate([weight_high, weight_high, weight_low], axis=0),
            preferred_element_type=F32,
        )
        result = jnp.maximum(projected, 0.0)
        if layer == 0:
            rows = result.astype(BF16)
        else:
            out[...] = result

    for layer in range(2):
        sent = stripe.at[layer, pl.ds(0, size - 1)]
        pltpu.make_async_copy(sent, sent, send_sem.at[layer]).wait()
        for entry in range(len(OFFSETS)):
            pltpu.make_async_remote_copy(
                src_ref=spare.at[layer],
                dst_ref=fetched.at[layer, entry],
                send_sem=near_send.at[layer, entry],
                recv_sem=near_recv.at[layer, entry],
                device_id=(readers[entry],),
                device_id_type=MESH,
            ).wait_send()


def shards(
    size, features, weight_one, weight_two, dense_tiles, dense_row, hub_block,
    sparse_tiles, sparse_row, sparse_src, sparse_count, fetch_list,
):
    slots = sparse_tiles.shape[0]
    nodes = features.shape[0]
    near = len(OFFSETS)
    smem = pl.BlockSpec(memory_space=pltpu.SMEM)
    hbm = pl.BlockSpec(memory_space=pl.ANY)
    return pl.pallas_call(
        functools.partial(kernel, size, slots),
        out_shape=jax.ShapeDtypeStruct((nodes, F), F32),
        in_specs=[smem] * 6 + [hbm] * 5,
        out_specs=pl.BlockSpec(memory_space=pltpu.VMEM),
        scratch_shapes=[
            pltpu.VMEM((nodes, F), F32),
            pltpu.VMEM((2, F, F), F32),
            pltpu.VMEM(dense_tiles.shape, BF16),
            pltpu.VMEM(sparse_tiles.shape, BF16),
            pltpu.VMEM((2, TILE, F), BF16),
            pltpu.VMEM((2, TILE, F), BF16),
            pltpu.VMEM((2, size, TILE, F), BF16),
            pltpu.VMEM((2, near, TILE, F), BF16),
            pltpu.VMEM((2 * (2 + near) + 1, TILE, 2 * F), BF16),
            pltpu.VMEM((TILE, 2 * F), F32),
            pltpu.SemaphoreType.DMA((5,)),
            pltpu.SemaphoreType.DMA((2,)),
            pltpu.SemaphoreType.DMA((2, size)),
            pltpu.SemaphoreType.DMA((2, near)),
            pltpu.SemaphoreType.DMA((2, near)),
        ],
        compiler_params=pltpu.CompilerParams(
            collective_id=0, has_side_effects=True, vmem_limit_bytes=56 * 2**20
        ),
    )(
        dense_row, hub_block, sparse_row, sparse_src, sparse_count, fetch_list,
        features, weight_one, weight_two, dense_tiles, sparse_tiles,
    )


def solution(mesh):
    size = mesh.shape["blk"]
    placed = (
        P("blk", None),
        P(),
        P(),
        P("blk", None, None),
        P("blk"),
        P(),
        P("blk", None, None),
        P("blk"),
        P("blk"),
        P("blk"),
        P("blk", None),
    )
    return jax.shard_map(
        functools.partial(shards, size),
        mesh=mesh, in_specs=placed, out_specs=P("blk", None), check_vma=False,
    )
```

```python
import functools
import math

import jax
import jax.numpy as jnp
from jax import lax
from jax.experimental import pallas as pl
from jax.experimental.pallas import tpu as pltpu
from jax.sharding import PartitionSpec as P

F = 128
TILE = 128
HOPS = 2
OFFSETS = list(range(-HOPS, 0)) + list(range(1, HOPS + 1))
MESH = pl.DeviceIdType.MESH
DIRECT = ()
BF16 = jnp.bfloat16
F32 = jnp.float32


def plane_side(chips):
    side = 1
    while chips % ((2 * side) ** 2) == 0 and 2 * (2 * side) ** 3 <= chips:
        side *= 2
    return side


def kernel(
    size, slots,
    dense_row, hub_block, sparse_count, fetch_list, sparse_row, sparse_src,
    features, weight_one, weight_two, dense_hbm, sparse_hbm,
    out,
    feat, weights, dense, sparse, spare, stripe, fetched, sums, adjacency, near_blocks,
    acc, lists, order, load_sem, send_sem, recv_sem, near_send, near_recv,
):
    side = plane_side(size // 2)
    long = size // (2 * side * side)
    me = lax.axis_index("blk")
    core = me % 2
    x = (me // 2) % side
    y = (me // (2 * side)) % side
    z = me // (2 * side * side)
    z_stride = 2 * side * side
    def at(dx, dy, dz, other=0):
        return (
            me
            + ((x + dx) % side - x) * 2
            + ((y + dy) % side - y) * 2 * side
            + ((z + dz) % long - z) * z_stride
            + other * (1 - 2 * core)
        )

    plane = [(dx, dy) for dy in range(side) for dx in range(side)][1:]
    direct = [dz for dz in DIRECT if dz < long]
    relayed = [dz for dz in range(1, long) if dz not in direct]
    twin = at(0, 0, 0, 1)
    owners = [(me + offset + size) % size for offset in OFFSETS]
    readers = [(me - offset + size) % size for offset in OFFSETS]

    barrier = pltpu.get_barrier_semaphore()
    partners = [at(0, 0, dz) for dz in range(1, long)] + [twin] + owners
    partners += [at(dx, dy, 0) for dx, dy in plane]
    for dz in direct:
        partners += [at(dx, dy, dz) for dx, dy in plane]
        partners += [at(dx, dy, -dz) for dx, dy in plane]
    for peer in partners:
        pl.semaphore_signal(barrier, inc=1, device_id=(peer,), device_id_type=MESH)

    loads = [
        pltpu.make_async_copy(features, feat, load_sem.at[0]),
        pltpu.make_async_copy(dense_hbm, dense, load_sem.at[1]),
        pltpu.make_async_copy(sparse_hbm, sparse, load_sem.at[2]),
        pltpu.make_async_copy(weight_one, weights.at[0], load_sem.at[3]),
        pltpu.make_async_copy(weight_two, weights.at[1], load_sem.at[4]),
    ]
    for load in loads:
        load.start()

    hub_here = hub_block[me]

    pairs = 2 * (2 + len(OFFSETS))
    row_wise = lax.broadcasted_iota(jnp.int32, (slots, slots), 0)
    lane_wise = lax.broadcasted_iota(jnp.int32, (slots, slots), 1)
    places = lax.broadcasted_iota(jnp.int32, (1, slots), 1)
    keys = jnp.where(places < sparse_count[0], 2 * sparse_src[...] + sparse_row[...], pairs)
    keys = jnp.broadcast_to(keys, (slots, slots))
    key_of_row = jnp.sum(jnp.where(row_wise == lane_wise, keys, 0), axis=1, keepdims=True)
    ahead = (keys < key_of_row) | ((keys == key_of_row) & (lane_wise < row_wise))
    rank = jnp.sum(jnp.where(ahead, 1, 0), axis=1, keepdims=True)
    lists[0:1, 0:slots] = jnp.sum(jnp.where(rank == lane_wise, row_wise, 0), axis=0, keepdims=True)
    lists[1:2, 0:slots] = jnp.sum(jnp.where(key_of_row < lane_wise, 1, 0), axis=0, keepdims=True)
    to_scalars = pltpu.make_async_copy(lists, order, load_sem.at[5])
    to_scalars.start()
    group = math.gcd(slots, 8)

    loads[0].wait()
    for layer in range(2):
        if layer == 0:
            rows = feat[...].astype(BF16)
        first, second = rows[:TILE], rows[TILE:]
        stripe[layer, me] = jnp.where(hub_here == 0, first, second)
        spare[layer] = jnp.where(hub_here == 0, second, first)
        near_blocks[0:TILE] = first
        near_blocks[TILE : 2 * TILE] = second
        if layer == 0:
            pl.semaphore_wait(barrier, len(partners))

        def copy(block, peer):
            return pltpu.make_async_remote_copy(
                src_ref=stripe.at[layer, block],
                dst_ref=stripe.at[layer, block],
                send_sem=send_sem.at[layer],
                recv_sem=recv_sem.at[layer, block],
                device_id=(peer,),
                device_id_type=MESH,
            )

        def near(entry):
            return pltpu.make_async_remote_copy(
                src_ref=spare.at[layer],
                dst_ref=fetched.at[layer, entry],
                send_sem=near_send.at[layer, entry],
                recv_sem=near_recv.at[layer, entry],
                device_id=(readers[entry],),
                device_id_type=MESH,
            )

        def arrive(block):
            copy(block, twin).wait_recv()

        def dense_group(dx, dy, other):
            blocks = [at(dx, dy, dz, other) for dz in range(long)]
            left = jnp.concatenate([dense[block] for block in blocks], axis=1)
            right = []
            for block in blocks:
                held = stripe[layer, block]
                row = dense_row[block]
                blank = jnp.zeros_like(held)
                right.append(
                    jnp.concatenate(
                        [jnp.where(row == 0, held, blank), jnp.where(row == 1, held, blank)], axis=1
                    )
                )
            acc[...] += jnp.dot(left, jnp.concatenate(right, axis=0), preferred_element_type=F32)

        for dz in relayed:
            copy(me, at(0, 0, dz)).start()
        for dx, dy in plane:
            copy(me, at(dx, dy, 0)).start()
        for dz in direct:
            for dx, dy in [(0, 0)] + plane:
                copy(me, at(dx, dy, dz)).start()
        copy(me, twin).start()
        for entry in range(len(OFFSETS)):
            near(entry).start()
        acc[...] = jnp.zeros_like(acc)

        for dz in relayed:
            block = at(0, 0, -dz)
            arrive(block)
            for dx, dy in plane:
                copy(block, at(dx, dy, 0)).start()
            copy(block, twin).start()
        for dx, dy in plane:
            block = at(dx, dy, 0)
            arrive(block)
            copy(block, twin).start()
        for dz in direct:
            for dx, dy in [(0, 0)] + plane:
                block = at(dx, dy, -dz)
                arrive(block)
                copy(block, twin).start()

        if layer == 0:
            loads[1].wait()
            loads[2].wait()
            to_scalars.wait()
            sums[0] = jnp.zeros((TILE, TILE), F32)

            @pl.loop(0, slots // group)
            def _(step):
                running = sums[step * group]
                for inner in range(group):
                    place = step * group + inner
                    running = running + sparse[order[0, place]].astype(F32)
                    sums[place + 1] = running

            for pair in range(pairs):
                source, row = pair // 2, pair % 2
                total = sums[order[1, pair + 1]] - sums[order[1, pair]]
                high = total.astype(BF16)
                low = (total - high.astype(F32)).astype(BF16)
                here = pl.ds(row * TILE, TILE)
                adjacency[0, here, source * TILE : (source + 1) * TILE] = high
                adjacency[1, here, source * TILE : (source + 1) * TILE] = low
        dense_group(0, 0, 0)

        for dx, dy in plane:
            for dz in relayed:
                block = at(dx, dy, -dz)
                arrive(block)
                copy(block, twin).start()
        for dx, dy in plane:
            dense_group(dx, dy, 0)

        for dx, dy in [(0, 0)] + plane:
            for dz in range(long):
                arrive(at(dx, dy, dz, 1))
            dense_group(dx, dy, 1)

        for entry in range(len(OFFSETS)):
            near(entry).wait_recv()
            owner = owners[entry]
            near_blocks[(entry + 2) * TILE : (entry + 3) * TILE] = jnp.where(
                fetch_list[0, entry] == hub_block[owner], stripe[layer, owner], fetched[layer, entry]
            )
        blocks = near_blocks[...]
        summed = jnp.concatenate([acc[:, :F], acc[:, F:]], axis=0)
        summed += jnp.dot(adjacency[0], blocks, preferred_element_type=F32)
        summed += jnp.dot(adjacency[1], blocks, preferred_element_type=F32)

        if layer == 0:
            loads[3].wait()
            loads[4].wait()
        weight = weights[layer]
        high = summed.astype(BF16)
        low = (summed - high.astype(F32)).astype(BF16)
        weight_high = weight.astype(BF16)
        weight_low = (weight - weight_high.astype(F32)).astype(BF16)
        projected = jnp.dot(
            jnp.concatenate([high, low, high], axis=1),
            jnp.concatenate([weight_high, weight_high, weight_low], axis=0),
            preferred_element_type=F32,
        )
        result = jnp.maximum(projected, 0.0)
        if layer == 0:
            rows = result.astype(BF16)
        else:
            out[...] = result

    for layer in range(2):
        sent = stripe.at[layer, pl.ds(0, size - 1)]
        pltpu.make_async_copy(sent, sent, send_sem.at[layer]).wait()
        for entry in range(len(OFFSETS)):
            pltpu.make_async_remote_copy(
                src_ref=spare.at[layer],
                dst_ref=fetched.at[layer, entry],
                send_sem=near_send.at[layer, entry],
                recv_sem=near_recv.at[layer, entry],
                device_id=(readers[entry],),
                device_id_type=MESH,
            ).wait_send()


def shards(
    size, features, weight_one, weight_two, dense_tiles, dense_row, hub_block,
    sparse_tiles, sparse_row, sparse_src, sparse_count, fetch_list,
):
    slots = sparse_tiles.shape[0]
    nodes = features.shape[0]
    near = len(OFFSETS)
    smem = pl.BlockSpec(memory_space=pltpu.SMEM)
    vmem = pl.BlockSpec(memory_space=pltpu.VMEM)
    hbm = pl.BlockSpec(memory_space=pl.ANY)
    return pl.pallas_call(
        functools.partial(kernel, size, slots),
        out_shape=jax.ShapeDtypeStruct((nodes, F), F32),
        in_specs=[smem] * 4 + [vmem] * 2 + [hbm] * 5,
        out_specs=vmem,
        scratch_shapes=[
            pltpu.VMEM((nodes, F), F32),
            pltpu.VMEM((2, F, F), F32),
            pltpu.VMEM(dense_tiles.shape, BF16),
            pltpu.VMEM(sparse_tiles.shape, BF16),
            pltpu.VMEM((2, TILE, F), BF16),
            pltpu.VMEM((2, size, TILE, F), BF16),
            pltpu.VMEM((2, near, TILE, F), BF16),
            pltpu.VMEM((slots + 1, TILE, TILE), F32),
            pltpu.VMEM((2, 2 * TILE, (2 + near) * TILE), BF16),
            pltpu.VMEM(((2 + near) * TILE, F), BF16),
            pltpu.VMEM((TILE, 2 * F), F32),
            pltpu.VMEM((8, 128), jnp.int32),
            pltpu.SMEM((8, 128), jnp.int32),
            pltpu.SemaphoreType.DMA((6,)),
            pltpu.SemaphoreType.DMA((2,)),
            pltpu.SemaphoreType.DMA((2, size)),
            pltpu.SemaphoreType.DMA((2, near)),
            pltpu.SemaphoreType.DMA((2, near)),
        ],
        compiler_params=pltpu.CompilerParams(
            collective_id=0, has_side_effects=True, vmem_limit_bytes=56 * 2**20
        ),
    )(
        dense_row, hub_block, sparse_count, fetch_list,
        sparse_row.reshape(1, slots), sparse_src.reshape(1, slots),
        features, weight_one, weight_two, dense_tiles, sparse_tiles,
    )


def solution(mesh):
    size = mesh.shape["blk"]
    placed = (
        P("blk", None),
        P(),
        P(),
        P("blk", None, None),
        P("blk"),
        P(),
        P("blk", None, None),
        P("blk"),
        P("blk"),
        P("blk"),
        P("blk", None),
    )
    return jax.shard_map(
        functools.partial(shards, size),
        mesh=mesh, in_specs=placed, out_specs=P("blk", None), check_vma=False,
    )
```

```python
import functools
import math

import jax
import jax.numpy as jnp
from jax import lax
from jax.experimental import pallas as pl
from jax.experimental.pallas import tpu as pltpu
from jax.sharding import PartitionSpec as P

F = 128
TILE = 128
HOPS = 2
OFFSETS = list(range(-HOPS, 0)) + list(range(1, HOPS + 1))
MESH = pl.DeviceIdType.MESH
DIRECT = ()
BF16 = jnp.bfloat16
F32 = jnp.float32


def plane_side(chips):
    side = 1
    while chips % ((2 * side) ** 2) == 0 and 2 * (2 * side) ** 3 <= chips:
        side *= 2
    return side


def kernel(
    size, slots,
    dense_row, hub_block, sparse_count, fetch_list, sparse_row, sparse_src,
    features, weight_one, weight_two, dense_hbm, sparse_hbm,
    out,
    feat, weights, dense, sparse, spare, stripe, fetched, sums, adjacency, near_blocks,
    acc, lists, order, load_sem, send_sem, recv_sem, near_send, near_recv,
):
    side = plane_side(size // 2)
    long = size // (2 * side * side)
    me = lax.axis_index("blk")
    core = me % 2
    x = (me // 2) % side
    y = (me // (2 * side)) % side
    z = me // (2 * side * side)
    z_stride = 2 * side * side
    def at(dx, dy, dz, other=0):
        return (
            me
            + ((x + dx) % side - x) * 2
            + ((y + dy) % side - y) * 2 * side
            + ((z + dz) % long - z) * z_stride
            + other * (1 - 2 * core)
        )

    plane = [(dx, dy) for dy in range(side) for dx in range(side)][1:]
    direct = [dz for dz in DIRECT if dz < long]
    relayed = [dz for dz in range(1, long) if dz not in direct]
    twin = at(0, 0, 0, 1)
    owners = [(me + offset + size) % size for offset in OFFSETS]
    far = [0, len(OFFSETS) - 1]
    relay_entry = 3 * (1 - core)

    barrier = pltpu.get_barrier_semaphore()
    partners = [at(0, 0, dz) for dz in range(1, long)] + [twin]
    partners += [owners[entry] for entry in far]
    partners += [at(dx, dy, 0) for dx, dy in plane]
    for dz in direct:
        partners += [at(dx, dy, dz) for dx, dy in plane]
        partners += [at(dx, dy, -dz) for dx, dy in plane]
    for peer in partners:
        pl.semaphore_signal(barrier, inc=1, device_id=(peer,), device_id_type=MESH)

    loads = [
        pltpu.make_async_copy(features, feat, load_sem.at[0]),
        pltpu.make_async_copy(dense_hbm, dense, load_sem.at[1]),
        pltpu.make_async_copy(sparse_hbm, sparse, load_sem.at[2]),
        pltpu.make_async_copy(weight_one, weights.at[0], load_sem.at[3]),
        pltpu.make_async_copy(weight_two, weights.at[1], load_sem.at[4]),
    ]
    for load in loads:
        load.start()

    hub_here = hub_block[me]

    pairs = 2 * (2 + len(OFFSETS))
    row_wise = lax.broadcasted_iota(jnp.int32, (slots, slots), 0)
    lane_wise = lax.broadcasted_iota(jnp.int32, (slots, slots), 1)
    places = lax.broadcasted_iota(jnp.int32, (1, slots), 1)
    keys = jnp.where(places < sparse_count[0], 2 * sparse_src[...] + sparse_row[...], pairs)
    keys = jnp.broadcast_to(keys, (slots, slots))
    key_of_row = jnp.sum(jnp.where(row_wise == lane_wise, keys, 0), axis=1, keepdims=True)
    ahead = (keys < key_of_row) | ((keys == key_of_row) & (lane_wise < row_wise))
    rank = jnp.sum(jnp.where(ahead, 1, 0), axis=1, keepdims=True)
    lists[0:1, 0:slots] = jnp.sum(jnp.where(rank == lane_wise, row_wise, 0), axis=0, keepdims=True)
    lists[1:2, 0:slots] = jnp.sum(jnp.where(key_of_row < lane_wise, 1, 0), axis=0, keepdims=True)
    to_scalars = pltpu.make_async_copy(lists, order, load_sem.at[5])
    to_scalars.start()
    group = math.gcd(slots, 8)

    loads[0].wait()
    for layer in range(2):
        if layer == 0:
            rows = feat[...].astype(BF16)
        first, second = rows[:TILE], rows[TILE:]
        stripe[layer, me] = jnp.where(hub_here == 0, first, second)
        spare[layer] = jnp.where(hub_here == 0, second, first)
        near_blocks[0:TILE] = first
        near_blocks[TILE : 2 * TILE] = second
        if layer == 0:
            pl.semaphore_wait(barrier, len(partners))

        def copy(block, peer):
            return pltpu.make_async_remote_copy(
                src_ref=stripe.at[layer, block],
                dst_ref=stripe.at[layer, block],
                send_sem=send_sem.at[layer],
                recv_sem=recv_sem.at[layer, block],
                device_id=(peer,),
                device_id_type=MESH,
            )

        def near(source, entry, peer, sem):
            return pltpu.make_async_remote_copy(
                src_ref=source,
                dst_ref=fetched.at[layer, entry],
                send_sem=near_send.at[layer, sem],
                recv_sem=near_recv.at[layer, entry],
                device_id=(peer,),
                device_id_type=MESH,
            )

        def near_arrive(entry):
            near(spare.at[layer], entry, twin, 0).wait_recv()

        def arrive(block):
            copy(block, twin).wait_recv()

        def dense_group(dx, dy, other):
            blocks = [at(dx, dy, dz, other) for dz in range(long)]
            left = jnp.concatenate([dense[block] for block in blocks], axis=1)
            right = []
            for block in blocks:
                held = stripe[layer, block]
                row = dense_row[block]
                blank = jnp.zeros_like(held)
                right.append(
                    jnp.concatenate(
                        [jnp.where(row == 0, held, blank), jnp.where(row == 1, held, blank)], axis=1
                    )
                )
            acc[...] += jnp.dot(left, jnp.concatenate(right, axis=0), preferred_element_type=F32)

        for dz in relayed:
            copy(me, at(0, 0, dz)).start()
        for dx, dy in plane:
            copy(me, at(dx, dy, 0)).start()
        for dz in direct:
            for dx, dy in [(0, 0)] + plane:
                copy(me, at(dx, dy, dz)).start()
        copy(me, twin).start()
        near(spare.at[layer], 0, owners[3], 0).start()
        near(spare.at[layer], 3, owners[0], 1).start()
        near(spare.at[layer], 1 + core, twin, 2).start()
        acc[...] = jnp.zeros_like(acc)

        for dz in relayed:
            block = at(0, 0, -dz)
            arrive(block)
            for dx, dy in plane:
                copy(block, at(dx, dy, 0)).start()
            copy(block, twin).start()
        for dx, dy in plane:
            block = at(dx, dy, 0)
            arrive(block)
            copy(block, twin).start()
        for dz in direct:
            for dx, dy in [(0, 0)] + plane:
                block = at(dx, dy, -dz)
                arrive(block)
                copy(block, twin).start()

        near_arrive(relay_entry)
        near(fetched.at[layer, relay_entry], 2 - core, twin, 3).start()

        if layer == 0:
            loads[1].wait()
            loads[2].wait()
            to_scalars.wait()
            sums[0] = jnp.zeros((TILE, TILE), F32)

            @pl.loop(0, slots // group)
            def _(step):
                running = sums[step * group]
                for inner in range(group):
                    place = step * group + inner
                    running = running + sparse[order[0, place]].astype(F32)
                    sums[place + 1] = running

            for pair in range(pairs):
                source, row = pair // 2, pair % 2
                total = sums[order[1, pair + 1]] - sums[order[1, pair]]
                high = total.astype(BF16)
                low = (total - high.astype(F32)).astype(BF16)
                here = pl.ds(row * TILE, TILE)
                adjacency[0, here, source * TILE : (source + 1) * TILE] = high
                adjacency[1, here, source * TILE : (source + 1) * TILE] = low
        dense_group(0, 0, 0)

        for dx, dy in plane:
            for dz in relayed:
                block = at(dx, dy, -dz)
                arrive(block)
                copy(block, twin).start()
        for dx, dy in plane:
            dense_group(dx, dy, 0)

        for dx, dy in [(0, 0)] + plane:
            for dz in range(long):
                arrive(at(dx, dy, dz, 1))
            dense_group(dx, dy, 1)

        near_arrive(3 - relay_entry)
        near_arrive(1)
        near_arrive(2)
        for entry in range(len(OFFSETS)):
            owner = owners[entry]
            near_blocks[(entry + 2) * TILE : (entry + 3) * TILE] = jnp.where(
                fetch_list[0, entry] == hub_block[owner], stripe[layer, owner], fetched[layer, entry]
            )
        blocks = near_blocks[...]
        summed = jnp.concatenate([acc[:, :F], acc[:, F:]], axis=0)
        summed += jnp.dot(adjacency[0], blocks, preferred_element_type=F32)
        summed += jnp.dot(adjacency[1], blocks, preferred_element_type=F32)

        if layer == 0:
            loads[3].wait()
            loads[4].wait()
        weight = weights[layer]
        high = summed.astype(BF16)
        low = (summed - high.astype(F32)).astype(BF16)
        weight_high = weight.astype(BF16)
        weight_low = (weight - weight_high.astype(F32)).astype(BF16)
        projected = jnp.dot(
            jnp.concatenate([high, low, high], axis=1),
            jnp.concatenate([weight_high, weight_high, weight_low], axis=0),
            preferred_element_type=F32,
        )
        if layer == 0:
            rows = jnp.maximum(projected, 0.0).astype(BF16)
        else:
            out[...] = projected

    for layer in range(2):
        sent = stripe.at[layer, pl.ds(0, size - 1)]
        pltpu.make_async_copy(sent, sent, send_sem.at[layer]).wait()
        for entry in range(len(OFFSETS)):
            pltpu.make_async_remote_copy(
                src_ref=spare.at[layer],
                dst_ref=fetched.at[layer, entry],
                send_sem=near_send.at[layer, entry],
                recv_sem=near_recv.at[layer, entry],
                device_id=(twin,),
                device_id_type=MESH,
            ).wait_send()


def shards(
    size, features, weight_one, weight_two, dense_tiles, dense_row, hub_block,
    sparse_tiles, sparse_row, sparse_src, sparse_count, fetch_list,
):
    slots = sparse_tiles.shape[0]
    nodes = features.shape[0]
    near = len(OFFSETS)
    smem = pl.BlockSpec(memory_space=pltpu.SMEM)
    vmem = pl.BlockSpec(memory_space=pltpu.VMEM)
    hbm = pl.BlockSpec(memory_space=pl.ANY)
    projected = pl.pallas_call(
        functools.partial(kernel, size, slots),
        out_shape=jax.ShapeDtypeStruct((nodes, F), F32),
        in_specs=[smem] * 4 + [vmem] * 2 + [hbm] * 5,
        out_specs=vmem,
        scratch_shapes=[
            pltpu.VMEM((nodes, F), F32),
            pltpu.VMEM((2, F, F), F32),
            pltpu.VMEM(dense_tiles.shape, BF16),
            pltpu.VMEM(sparse_tiles.shape, BF16),
            pltpu.VMEM((2, TILE, F), BF16),
            pltpu.VMEM((2, size, TILE, F), BF16),
            pltpu.VMEM((2, near, TILE, F), BF16),
            pltpu.VMEM((slots + 1, TILE, TILE), F32),
            pltpu.VMEM((2, 2 * TILE, (2 + near) * TILE), BF16),
            pltpu.VMEM(((2 + near) * TILE, F), BF16),
            pltpu.VMEM((TILE, 2 * F), F32),
            pltpu.VMEM((8, 128), jnp.int32),
            pltpu.SMEM((8, 128), jnp.int32),
            pltpu.SemaphoreType.DMA((6,)),
            pltpu.SemaphoreType.DMA((2,)),
            pltpu.SemaphoreType.DMA((2, size)),
            pltpu.SemaphoreType.DMA((2, near)),
            pltpu.SemaphoreType.DMA((2, near)),
        ],
        compiler_params=pltpu.CompilerParams(
            collective_id=0, has_side_effects=True, vmem_limit_bytes=56 * 2**20
        ),
    )(
        dense_row, hub_block, sparse_count, fetch_list,
        sparse_row.reshape(1, slots), sparse_src.reshape(1, slots),
        features, weight_one, weight_two, dense_tiles, sparse_tiles,
    )
    return jax.nn.relu(projected)


def solution(mesh):
    size = mesh.shape["blk"]
    placed = (
        P("blk", None),
        P(),
        P(),
        P("blk", None, None),
        P("blk"),
        P(),
        P("blk", None, None),
        P("blk"),
        P("blk"),
        P("blk"),
        P("blk", None),
    )
    return jax.shard_map(
        functools.partial(shards, size),
        mesh=mesh, in_specs=placed, out_specs=P("blk", None), check_vma=False,
    )
```
